32 devices in a mesh: img: 4 (over y, x), grp: 8 (over z, core).
Axes of the slice: x: 2, y: 2, z: 4, core: 2. Of those that a mesh axis runs over, the one named last changes fastest.
Arguments:
- glob_x: bfloat16 [128, 14, 14, 512], P(('img', 'grp')), may hold values from -6 to 6
- loc_x: bfloat16 [384, 7, 7, 512], P(('img', 'grp')), may hold values from -6 to 6
- glob_cot: bfloat16 [128, 14, 14, 512], P(('img', 'grp')), may hold values from -6 to 6
- loc_cot: bfloat16 [384, 7, 7, 512], P(('img', 'grp')), may hold values from -6 to 6
- loc_extent: int32 [384, 2], P(('img', 'grp')), may hold values from 3 to 7
- glob_image: int32 [128], P('img'), may hold values from 0 to 15, as said below
- loc_image: int32 [384], P('img'), may hold values from 0 to 15, as said below
- s_kernels: bfloat16 [2, 9, 512], replicated, may hold values from -2 to 2
- s_gains: bfloat16 [2, 512], replicated, may hold values from 0.5 to 1.5
- s_shifts: bfloat16 [8, 512], replicated, may hold values from -1.5 to 1.5
- s_qkv: bfloat16 [512, 1536], replicated, may hold values from -0.25 to 0.25
- s_proj: bfloat16 [512, 512], replicated, may hold values from -1.5 to 1.5
- s_fc1: bfloat16 [512, 2048], replicated, may hold values from -0.25 to 0.25
- s_fc1_bias: bfloat16 [2048], replicated, may hold values from -1.5 to 1.5
- s_fc2: bfloat16 [2048, 512], replicated, may hold values from -0.125 to 0.125
- c_kernels: bfloat16 [2, 9, 512], replicated, may hold values from -2 to 2
- c_gains: bfloat16 [2, 512], replicated, may hold values from 0.5 to 1.5
- c_shifts: bfloat16 [9, 512], replicated, may hold values from -1.5 to 1.5
- c_qkv: bfloat16 [512, 1536], replicated, may hold values from -0.25 to 0.25
- c_proj: bfloat16 [512, 512], replicated, may hold values from -1 to 1
- c_fc1: bfloat16 [512, 2048], replicated, may hold values from -0.25 to 0.25
- c_fc1_bias: bfloat16 [2048], replicated, may hold values from -1.5 to 1.5
- c_fc2: bfloat16 [2048, 512], replicated, may hold values from -0.125 to 0.125
Outputs:
- glob_out: bfloat16 [128, 14, 14, 512], P(('img', 'grp'))
- loc_out: bfloat16 [384, 7, 7, 512], P(('img', 'grp'))
- glob_grad: float32 [128, 14, 14, 512], P(('img', 'grp'))
- loc_grad: float32 [384, 7, 7, 512], P(('img', 'grp'))
- s_kernels_grad: float32 [2, 9, 512], P(None, None, 'grp')
- s_gains_grad: float32 [2, 512], P(None, 'grp')
- s_shifts_grad: float32 [8, 512], P(None, 'grp')
- s_qkv_grad: float32 [512, 1536], P(None, 'grp')
- s_proj_grad: float32 [512, 512], P(None, 'grp')
- s_fc1_grad: float32 [512, 2048], P(None, 'grp')
- s_fc1_bias_grad: float32 [2048], P('grp')
- s_fc2_grad: float32 [2048, 512], P(None, 'grp')
- c_kernels_grad: float32 [2, 9, 512], P(None, None, 'grp')
- c_gains_grad: float32 [2, 512], P(None, 'grp')
- c_shifts_grad: float32 [9, 512], P(None, 'grp')
- c_qkv_grad: float32 [512, 1536], P(None, 'grp')
- c_proj_grad: float32 [512, 512], P(None, 'grp')
- c_fc1_grad: float32 [512, 2048], P(None, 'grp')
- c_fc1_bias_grad: float32 [2048], P('grp')
- c_fc2_grad: float32 [2048, 512], P(None, 'grp')
The draws below stay inside these ranges and needn't reach their ends.
Inputs may be any that keep to these rules, and one draw needn't show every extreme that they name: `glob_image`: within each image row every one of its 16 images owns exactly 2 global crops. `loc_image`: within each image row every one of its 16 images owns exactly 6 local crops.
All inputs are finite; a program needn't handle non-finite values.
Results may differ from the reference program's by a relative error of at most 0.03.
Values may be sent and summed in bfloat16 or wider, within the bound.
No kernel may reach another device: no remote copies, remote signals or barrier semaphores. Data moves between devices by JAX's collectives and lax.ppermute only.
A program may use at most 320 MiB of HBM per device.

```python
import jax
import jax.numpy as jnp
from jax import lax

D = 512
HEADS = 16
HEAD_DIM = 32
FF = 2048
WIN = 7
ROW_IMAGES = 16
ROWS = 4
GLOB_TOTAL = 128
LOC_TOTAL = 384


def spread_images(key, copies):
    total_len = ROW_IMAGES * copies
    base_order = jnp.roll(jnp.repeat(jnp.arange(ROW_IMAGES, dtype=jnp.int32), copies), 1)

    def one_row(row_key):
        order_key, label_key = jax.random.split(row_key)
        inner = jax.random.permutation(order_key, total_len - 2).astype(jnp.int32) + 1
        order = jnp.concatenate([jnp.zeros((1,), jnp.int32), inner, jnp.full((1,), total_len - 1, jnp.int32)])
        labels = jax.random.permutation(label_key, ROW_IMAGES).astype(jnp.int32)
        return labels[base_order[order]]
    return jax.vmap(one_row)(jax.random.split(key, ROWS)).reshape(-1).astype(jnp.int32)


def draw_glob_image(key, part):
    key = jax.random.fold_in(key, 11)
    return spread_images(key, 2)


def draw_loc_image(key, part):
    key = jax.random.fold_in(key, 23)
    return spread_images(key, 6)


def with_ends(array, rng, low, high):
    place = [jax.random.randint(jax.random.fold_in(rng, axis), (), 0, length) for axis, length in enumerate(array.shape)]
    widest = array.shape.index(max(array.shape))
    neighbour = place[:widest] + [(place[widest] + 1) % array.shape[widest]] + place[widest + 1:]
    return array.at[tuple(place)].set(low).at[tuple(neighbour)].set(high)


def shard_levels(own_key, shape, cuts, least, largest):
    def one(dim, shards_of):
        steps = jax.random.uniform(jax.random.fold_in(jax.random.fold_in(own_key, 6), dim), (shards_of,), jnp.float32, least / len(cuts), largest / len(cuts))
        return jnp.repeat(jnp.exp(steps), shape[dim] // shards_of).reshape((-1,) + (1,) * (len(shape) - dim - 1))

    level = one(*cuts[0])
    for cut in cuts[1:]:
        level = level * one(*cut)
    return level


def scatter_about(rng, shape, spread, limit, cuts=(), kind=jnp.bfloat16):
    values = jax.random.normal(rng, shape, jnp.float32) * spread
    if len(cuts) > 0:
        values = shard_levels(rng, shape, cuts, -0.22, 0.18) * values
    return jnp.clip(values, min=-limit, max=limit).astype(kind)


def setup_inputs(seed: int = 0) -> dict:
    key_list = jax.random.split(jax.random.key(seed), 24)
    glob_x = scatter_about(key_list[0], (GLOB_TOTAL, 2 * WIN, 2 * WIN, D), 1.0, 6.0, ((0, 32),))
    loc_x = scatter_about(key_list[1], (LOC_TOTAL, WIN, WIN, D), 1.0, 6.0, ((0, 32),))
    glob_cot = scatter_about(key_list[2], (GLOB_TOTAL, 2 * WIN, 2 * WIN, D), 1.0, 6.0, ((0, 32),))
    loc_cot = scatter_about(key_list[3], (LOC_TOTAL, WIN, WIN, D), 1.0, 6.0, ((0, 32),))
    loc_extent = with_ends(jax.random.randint(key_list[4], (LOC_TOTAL, 2), 3, 8), jax.random.fold_in(key_list[4], 1), 3, 7).astype(jnp.int32)
    glob_image = draw_glob_image(jax.random.fold_in(key_list[23], 71), 0)
    loc_image = draw_loc_image(jax.random.fold_in(key_list[23], 71), 0)
    s_kernels = scatter_about(key_list[7], (2, 9, D), 9 ** -0.5, 2.0)
    s_gains = jnp.clip(1.0 + 0.1 * jax.random.normal(key_list[8], (2, D), jnp.float32), 0.5, 1.5).astype(jnp.bfloat16)
    s_shifts = scatter_about(key_list[9], (8, D), 0.3, 1.5)
    s_qkv = scatter_about(key_list[10], (D, 3 * D), D ** -0.5, 0.25)
    s_proj = scatter_about(key_list[11], (D, D), (max(D // 32, 1)) ** -0.5, 1.5)
    s_fc1 = scatter_about(key_list[12], (D, FF), D ** -0.5, 0.25)
    s_fc1_bias = scatter_about(key_list[13], (FF,), 0.3, 1.5)
    s_fc2 = scatter_about(key_list[14], (FF, D), FF ** -0.5, 0.125)
    c_kernels = scatter_about(key_list[15], (2, 9, D), 9 ** -0.5, 2.0)
    c_gains = jnp.clip(1.0 + 0.1 * jax.random.normal(key_list[16], (2, D), jnp.float32), 0.5, 1.5).astype(jnp.bfloat16)
    c_shifts = scatter_about(key_list[17], (9, D), 0.3, 1.5)
    c_qkv = scatter_about(key_list[18], (D, 3 * D), D ** -0.5, 0.25)
    c_proj = scatter_about(key_list[19], (D, D), (max(D // 16, 1)) ** -0.5, 1.0)
    c_fc1 = scatter_about(key_list[20], (D, FF), D ** -0.5, 0.25)
    c_fc1_bias = scatter_about(key_list[21], (FF,), 0.3, 1.5)
    c_fc2 = scatter_about(key_list[22], (FF, D), FF ** -0.5, 0.125)
    return dict(glob_x=glob_x, loc_x=loc_x, glob_cot=glob_cot, loc_cot=loc_cot, loc_extent=loc_extent, glob_image=glob_image, loc_image=loc_image, s_kernels=s_kernels, s_gains=s_gains, s_shifts=s_shifts, s_qkv=s_qkv, s_proj=s_proj, s_fc1=s_fc1, s_fc1_bias=s_fc1_bias, s_fc2=s_fc2, c_kernels=c_kernels, c_gains=c_gains, c_shifts=c_shifts, c_qkv=c_qkv, c_proj=c_proj, c_fc1=c_fc1, c_fc1_bias=c_fc1_bias, c_fc2=c_fc2)


PRECISE = lax.Precision.HIGHEST
EPSILON = 1e-05
MASK_FILL = 1000000000.0

@jax.custom_vjp
def low(v):
    return lax.optimization_barrier(v.astype(jnp.bfloat16)).astype(jnp.float32)

@jax.custom_vjp
def low_back(v):
    return v

def low_keep(v):
    return (low(v), None)

def low_pass(kept, grad):
    return (grad,)

def back_keep(v):
    return (v, None)

def back_low(kept, grad):
    return (low(grad),)
low.defvjp(low_keep, low_pass)
low_back.defvjp(back_keep, back_low)

def channel_scale():
    return (14 * WIN * WIN) ** (-0.5)

def matmul_hi(left_op, right_op):
    return jnp.dot(left_op, right_op, precision=PRECISE, preferred_element_type=jnp.float32)

def to_tokens(glob_maps, loc_maps):
    channels = glob_maps.shape[-1]
    crop_count = glob_maps.shape[0]
    tiles = glob_maps.reshape(crop_count, 2, WIN, 2, WIN, channels).transpose(0, 1, 3, 2, 4, 5)
    return jnp.concatenate([tiles.reshape(-1, channels), loc_maps.reshape(-1, channels)], axis=0)

def to_maps(tokens, crop_count):
    channels = tokens.shape[-1]
    split_at = crop_count * 4 * WIN * WIN
    tiles = tokens[:split_at].reshape(crop_count, 2, 2, WIN, WIN, channels).transpose(0, 1, 3, 2, 4, 5)
    return (tiles.reshape(crop_count, 2 * WIN, 2 * WIN, channels), tokens[split_at:].reshape(-1, WIN, WIN, channels))

def depthwise(map_data, kernel, offset):
    map_side = map_data.shape[1]
    padded = jnp.pad(map_data, ((0, 0), (1, 1), (1, 1), (0, 0)))
    result = jnp.zeros_like(map_data) + offset
    for tap_row in range(3):
        for tap_col in range(3):
            result = result + padded[:, tap_row:tap_row + map_side, tap_col:tap_col + map_side, :] * kernel[3 * tap_row + tap_col]
    return result

def conv_add(tokens, valid_mask, kernel, offset, crop_count):
    glob_maps, loc_maps = to_maps(tokens * valid_mask[:, None], crop_count)
    return tokens + to_tokens(depthwise(glob_maps, kernel, offset), depthwise(loc_maps, kernel, offset))

def layer_norm(tokens, gain_vec, offset):
    centered = tokens - lax.optimization_barrier(jnp.mean(tokens, axis=-1, keepdims=True))
    variance = lax.optimization_barrier(jnp.mean(centered * centered, axis=-1, keepdims=True))
    return centered * lax.rsqrt(variance + EPSILON) * gain_vec + offset

def softmax(scores):
    exponent = jnp.exp(scores - lax.optimization_barrier(jnp.max(scores, axis=-1, keepdims=True)))
    return exponent / lax.optimization_barrier(jnp.sum(exponent, axis=-1, keepdims=True))

def gelu_exact(inputs):
    return 0.5 * inputs * (1.0 + lax.erf(inputs * 0.7071067811865476))

def local_mask(extent):
    cell_index = jnp.arange(WIN, dtype=jnp.int32)
    inside = (cell_index[None, :, None] < extent[:, 0, None, None]) & (cell_index[None, None, :] < extent[:, 1, None, None])
    return inside.astype(jnp.float32).reshape(-1)

def window_attend(queries, keys_in, values, key_bias):
    scores = jnp.einsum('wnhc,wmhc->whnm', queries, keys_in, precision=PRECISE) * HEAD_DIM ** (-0.5)
    scores = low_back(scores + key_bias[:, None, None, :])
    attn_probs = low(softmax(scores))
    result = jnp.einsum('whnm,wmhc->wnhc', attn_probs, values, precision=PRECISE)
    return low(low_back(result))

def channel_attend(queries, keys_in, values, valid_mask, window_image):
    masked = queries * valid_mask[:, :, None, None]
    gram_sums = jnp.einsum('wnhc,wnhd->whcd', masked, keys_in, precision=PRECISE)
    scores = jax.ops.segment_sum(gram_sums, window_image, num_segments=ROW_IMAGES) * channel_scale()
    attn_probs = low(softmax(low_back(scores)))
    result = jnp.einsum('whcd,wnhd->wnhc', attn_probs[window_image], values, precision=PRECISE)
    return low(low_back(result))

def block(tokens, valid_mask, key_bias, window_image, crop_count, params, spatial):
    kernels, gain_rows, shifts, qkv_weight, proj_weight, fc1_weight, fc1_bias, fc2_weight = params
    channels = tokens.shape[-1]
    if spatial:
        qkv_bias = jnp.concatenate([shifts[4], jnp.zeros_like(shifts[4]), shifts[5]])
        proj_bias, fc2_bias = (shifts[6], shifts[7])
    else:
        qkv_bias = shifts[4:7].reshape(-1)
        proj_bias, fc2_bias = (shifts[7], shifts[8])
    section_one = conv_add(tokens, valid_mask, kernels[0], shifts[0], crop_count)
    normed = low(layer_norm(section_one, gain_rows[0], shifts[2]))
    projected = low(low_back(matmul_hi(normed, qkv_weight) + qkv_bias))
    windows = projected.shape[0] // (WIN * WIN)
    queries, keys_in, values = [projected[:, third_idx * channels:(third_idx + 1) * channels].reshape(windows, WIN * WIN, HEADS, HEAD_DIM) for third_idx in range(3)]
    if spatial:
        attended = window_attend(queries, keys_in, values, key_bias)
    else:
        attended = channel_attend(queries, keys_in, values, valid_mask.reshape(windows, WIN * WIN), window_image)
    section_two = section_one + low_back(matmul_hi(attended.reshape(-1, channels), proj_weight) + proj_bias)
    section_three = conv_add(section_two, valid_mask, kernels[1], shifts[1], crop_count)
    normed_two = low(layer_norm(section_three, gain_rows[1], shifts[3]))
    hidden_pre = low_back(matmul_hi(normed_two, fc1_weight) + fc1_bias)
    activated = low(gelu_exact(hidden_pre))
    return section_three + low_back(matmul_hi(activated, fc2_weight) + fc2_bias)

def reference(glob_x, loc_x, glob_cot, loc_cot, loc_extent, glob_image, loc_image, s_kernels, s_gains, s_shifts, s_qkv, s_proj, s_fc1, s_fc1_bias, s_fc2, c_kernels, c_gains, c_shifts, c_qkv, c_proj, c_fc1, c_fc1_bias, c_fc2):
    weights = tuple((member.astype(jnp.float32) for member in (s_kernels, s_gains, s_shifts, s_qkv, s_proj, s_fc1, s_fc1_bias, s_fc2, c_kernels, c_gains, c_shifts, c_qkv, c_proj, c_fc1, c_fc1_bias, c_fc2)))
    glob_count = 2 * ROW_IMAGES
    local_count = 6 * ROW_IMAGES
    row_inputs = (glob_x.reshape(ROWS, glob_count, 2 * WIN, 2 * WIN, D), loc_x.reshape(ROWS, local_count, WIN, WIN, D), glob_cot.reshape(ROWS, glob_count, 2 * WIN, 2 * WIN, D), loc_cot.reshape(ROWS, local_count, WIN, WIN, D), loc_extent.reshape(ROWS, local_count, 2), glob_image.reshape(ROWS, glob_count), loc_image.reshape(ROWS, local_count))

    def row_step(totals, row_item):
        glob_row, loc_row, glob_cot_row, loc_cot_row, extent, glob_ids, loc_ids = row_item
        valid_mask = jnp.concatenate([jnp.ones((glob_count * 4 * WIN * WIN,), jnp.float32), local_mask(extent)])
        key_bias = (valid_mask.reshape(-1, WIN * WIN) - 1.0) * MASK_FILL
        window_image = jnp.concatenate([jnp.repeat(glob_ids, 4), loc_ids]).astype(jnp.int32)

        def forward(glob_in, loc_in, *params):
            tokens = to_tokens(glob_in, loc_in)
            middle = block(tokens, valid_mask, key_bias, window_image, glob_count, params[:8], True)
            output = block(middle, valid_mask, key_bias, window_image, glob_count, params[8:], False)
            return to_maps(output, glob_count)
        row_outs, pull_back = jax.vjp(forward, glob_row.astype(jnp.float32), loc_row.astype(jnp.float32), *weights)
        gradients = pull_back((glob_cot_row.astype(jnp.float32), loc_cot_row.astype(jnp.float32)))
        totals = tuple((acc_val + new_val for acc_val, new_val in zip(totals, gradients[2:])))
        return (totals, (row_outs[0].astype(jnp.bfloat16), row_outs[1].astype(jnp.bfloat16), gradients[0], gradients[1]))
    zero_grads = tuple((jnp.zeros_like(member) for member in weights))
    totals, (glob_rows, loc_rows, glob_grads, loc_grads) = lax.scan(row_step, zero_grads, row_inputs)
    return (glob_rows.reshape(GLOB_TOTAL, 2 * WIN, 2 * WIN, D), loc_rows.reshape(LOC_TOTAL, WIN, WIN, D), glob_grads.reshape(GLOB_TOTAL, 2 * WIN, 2 * WIN, D), loc_grads.reshape(LOC_TOTAL, WIN, WIN, D), totals[0], totals[1], totals[2], totals[3], totals[4], totals[5], totals[6], totals[7], totals[8], totals[9], totals[10], totals[11], totals[12], totals[13], totals[14], totals[15])
```

```python
import functools

import jax
import jax.numpy as jnp
from jax import lax
from jax.experimental import pallas as pl
from jax.experimental.pallas import tpu as pltpu
from jax.sharding import PartitionSpec as P

F32 = jnp.float32
BF16 = jnp.bfloat16
HEAD_DIM = 32
WIN = 7
COLS = 8
TOK = WIN * COLS
WPC = 4
LINES = WPC * WIN
CHUNK = WPC * TOK
LANES = 128
EPSILON = 1e-05
MASK_FILL = 1000000000.0
VMEM = 56 * 1024 * 1024
GRP = ("line", "core")


def nn(a, b):
    return lax.dot_general(a, b, (((1,), (0,)), ((), ())), preferred_element_type=F32)


def nt(a, b):
    return lax.dot_general(a, b, (((1,), (1,)), ((), ())), preferred_element_type=F32)


def tn(a, b):
    return lax.dot_general(a, b, (((0,), (0,)), ((), ())), preferred_element_type=F32)


def channel_scale():
    return (14 * WIN * WIN) ** (-0.5)


def lane_slices(width):
    return [slice(s, s + LANES) for s in range(0, width, LANES)]


def head_mask(rows, head, dtype):
    lane = lax.broadcasted_iota(jnp.int32, (rows, LANES), 1)
    return jnp.where(lane // HEAD_DIM == head, 1.0, 0.0).astype(dtype)


def block_mask(dtype):
    row = lax.broadcasted_iota(jnp.int32, (LANES, LANES), 0)
    lane = lax.broadcasted_iota(jnp.int32, (LANES, LANES), 1)
    return jnp.where(row // HEAD_DIM == lane // HEAD_DIM, 1.0, 0.0).astype(dtype)


class Where:
    def __init__(self, globs, chunk, place, glob_image, loc_image, extent):
        self.globs, self.chunk, self.place = globs, chunk, place
        self.glob_image, self.loc_image, self.extent = glob_image, loc_image, extent
        self.is_glob = chunk < globs
        self.local = jnp.maximum(chunk - globs, 0) * WPC
        self.gate = jnp.where(self.is_glob, 1.0, 0.0)

    def sides(self, w):
        return [
            jnp.where(self.is_glob, WIN, self.extent[side, self.local + w]) for side in range(2)
        ]

    def image(self, w, images):
        core, line, lines_of = self.place[0], self.place[1], self.place[3]
        me = line * 2 + core
        locs = self.extent.shape[1]
        image = jnp.where(
            self.is_glob,
            self.glob_image[me * self.globs + jnp.minimum(self.chunk, self.globs - 1)],
            self.loc_image[me * locs + self.local + w],
        )
        per = images // (2 * lines_of)
        owner = image // per
        side = jnp.bitwise_xor(owner % 2, core) * lines_of
        return (side + jnp.bitwise_xor(owner // 2, line)) * per + image % per


def fill_valid(where, valid):
    for w in range(WPC):
        row = lax.broadcasted_iota(jnp.int32, (WIN, COLS, LANES), 0)
        col = lax.broadcasted_iota(jnp.int32, (WIN, COLS, LANES), 1)
        high, wide = where.sides(w)
        inside = (row < high) & (col < wide)
        valid[WIN * w : WIN * w + WIN] = jnp.where(inside, 1.0, 0.0)


def fill_vec(kernels, gains, shifts, vec):
    for t in range(9):
        both = kernels[t].astype(F32)
        vec[t : t + 1] = both[0:1]
        vec[9 + t : 10 + t] = both[1:2]
    vec[18:20] = gains[...].astype(F32)
    vec[20 : 20 + shifts.shape[0]] = shifts[...].astype(F32)


def load_tokens(chunk, globs, glob_ref, loc_ref, dst, wide):
    @pl.when(chunk < globs)
    def _():
        wide[:, 0:14, :] = glob_ref[0].astype(F32)
        for w in range(WPC):
            a, b = divmod(w, 2)
            tile = wide[WIN * a : WIN * a + WIN, pl.ds(WIN * b, COLS), :]
            col = lax.broadcasted_iota(jnp.int32, tile.shape, 1)
            dst[WIN * w : WIN * w + WIN] = jnp.where(col < WIN, tile, 0.0)

    @pl.when(chunk >= globs)
    def _():
        for w in range(WPC):
            dst[WIN * w : WIN * w + WIN, 0:WIN, :] = loc_ref[w].astype(F32)
        dst[:, WIN:COLS, :] = jnp.zeros((LINES, 1, dst.shape[2]), F32)


def store_tokens(chunk, globs, src, glob_ref, loc_ref, wide):
    @pl.when(chunk < globs)
    def _():
        for b in range(2):
            for a in range(2):
                w = 2 * a + b
                wide[WIN * a : WIN * a + WIN, pl.ds(WIN * b, COLS), :] = src[
                    WIN * w : WIN * w + WIN
                ]
        glob_ref[0] = wide[:, 0:14, :].astype(glob_ref.dtype)

    @pl.when(chunk >= globs)
    def _():
        for w in range(WPC):
            loc_ref[w] = src[WIN * w : WIN * w + WIN, 0:WIN, :].astype(loc_ref.dtype)


def shifted(tiles, gate):
    left = [pltpu.roll(t, 1, 1) for t in tiles]
    right = [pltpu.roll(t, COLS - 1, 1) for t in tiles]
    col = lax.broadcasted_iota(jnp.int32, tiles[0].shape, 1)
    for w in (1, 3):
        left[w] = jnp.where(col == 0, gate * pltpu.roll(left[w - 1], 1, 1), left[w])
    for w in (0, 2):
        right[w] = jnp.where(
            col == WIN - 1, gate * pltpu.roll(right[w + 1], COLS - 1, 1), right[w]
        )
    none = jnp.zeros((1, COLS, LANES), F32)
    result = []
    for kind in (left, tiles, right):
        result.append(
            [
                jnp.concatenate(
                    [
                        gate * kind[w - 2][WIN - 1 : WIN] if w >= 2 else none,
                        kind[w],
                        gate * kind[w + 2][0:1] if w < 2 else none,
                    ],
                    axis=0,
                )
                for w in range(WPC)
            ]
        )
    return result


def row_of(vec, row, lanes):
    return vec[row : row + 1, lanes].reshape(1, 1, LANES)


def conv_forward(src, valid, vec, kernel_row, bias_row, gate, dst):
    for lanes in lane_slices(src.shape[2]):
        tiles = [src[WIN * w : WIN * w + WIN, :, lanes] for w in range(WPC)]
        masked = [tiles[w] * valid[WIN * w : WIN * w + WIN] for w in range(WPC)]
        kinds = shifted(masked, gate)
        taps = [row_of(vec, kernel_row + t, lanes) for t in range(9)]
        bias = row_of(vec, bias_row, lanes)
        for w in range(WPC):
            total = tiles[w] + bias
            for i in range(3):
                for j in range(3):
                    total = total + kinds[j][w][i : i + WIN] * taps[3 * i + j]
            dst[WIN * w : WIN * w + WIN, :, lanes] = total


def conv_backward(grad, src, valid, vec, kernel_row, gate, dst, acc, acc_row, acc_bias_row):
    for lanes in lane_slices(src.shape[2]):
        tiles = [grad[WIN * w : WIN * w + WIN, :, lanes] for w in range(WPC)]
        kinds = shifted(tiles, gate)
        taps = [row_of(vec, kernel_row + t, lanes) for t in range(9)]
        sums = [None] * 9
        bias_sum = None
        for w in range(WPC):
            mask = valid[WIN * w : WIN * w + WIN]
            masked = src[WIN * w : WIN * w + WIN, :, lanes] * mask
            total = None
            for i in range(3):
                for j in range(3):
                    piece = kinds[2 - j][w][2 - i : 2 - i + WIN]
                    term = piece * taps[3 * i + j]
                    total = term if total is None else total + term
                    part = jnp.sum(piece * masked, axis=0)
                    t = 3 * i + j
                    sums[t] = part if sums[t] is None else sums[t] + part
            dst[WIN * w : WIN * w + WIN, :, lanes] = tiles[w] + total * mask
            part = jnp.sum(tiles[w], axis=0)
            bias_sum = part if bias_sum is None else bias_sum + part
        for t in range(9):
            acc[acc_row + t, :, lanes] += sums[t]
        acc[acc_bias_row, :, lanes] += bias_sum


def norm_blocks(src):
    width = src.shape[2]

    def block(b):
        return src[b : b + 4].reshape(4 * COLS, width)

    starts = range(0, LINES, 4)
    means = [jnp.mean(block(b), axis=-1, keepdims=True) for b in starts]
    spreads = []
    for b, mean in zip(starts, means):
        x = block(b) - mean
        spreads.append(jnp.mean(x * x, axis=-1, keepdims=True))
    scales = [lax.rsqrt(v + EPSILON) for v in spreads]
    return starts, block, means, scales


def norm_forward(src, vec, gain_row, shift_row, dst):
    gain = vec[gain_row : gain_row + 1, :]
    shift = vec[shift_row : shift_row + 1, :]
    starts, block, means, scales = norm_blocks(src)
    for b, mean, scale in zip(starts, means, scales):
        x = (block(b) - mean) * scale
        dst[b * COLS : (b + 4) * COLS, :] = (x * gain + shift).astype(BF16)


def norm_backward(grad, src, vec, gain_row, base, dst, acc, acc_gain, acc_shift):
    gain = vec[gain_row : gain_row + 1, :]
    width = src.shape[2]
    gain_sum = jnp.zeros((COLS, width), F32)
    shift_sum = jnp.zeros((COLS, width), F32)
    starts, block, means, scales = norm_blocks(src)
    sums = []
    for b, mean, scale in zip(starts, means, scales):
        x = (block(b) - mean) * scale
        g = grad[b * COLS : (b + 4) * COLS, :]
        gx = g * x
        gain_sum = gain_sum + jnp.sum(gx.reshape(4, COLS, width), axis=0)
        shift_sum = shift_sum + jnp.sum(g.reshape(4, COLS, width), axis=0)
        sums.append(
            (
                jnp.mean(g * gain, axis=-1, keepdims=True),
                jnp.mean(gx * gain, axis=-1, keepdims=True),
            )
        )
    for b, mean, scale, (mean_g, mean_gx) in zip(starts, means, scales, sums):
        x = (block(b) - mean) * scale
        g = grad[b * COLS : (b + 4) * COLS, :] * gain
        result = (g - mean_g - x * mean_gx) * scale
        dst[b : b + 4] = base[b : b + 4] + result.reshape(4, COLS, width)
    acc[acc_gain] += gain_sum
    acc[acc_shift] += shift_sum


def gelu_parts(u):
    phi = 0.5 + 0.5 * lax.erf(u * 0.7071067811865476)
    return u * phi, phi + u * (0.3989422804014327 * jnp.exp(-0.5 * u * u))


def column_sums(value, rows=CHUNK):
    return jnp.sum(value.reshape(rows // COLS, COLS, value.shape[1]), axis=0)


def feed_forward(h, w1, b1, act, slope):
    width = 512
    hidden = h[...]
    for s in range(0, w1.shape[1], width):
        u = nn(hidden, w1[:, s : s + width]) + b1[:, s : s + width].astype(F32)
        for r in range(0, CHUNK, 32):
            for c in range(0, width, 256):
                value, deriv = gelu_parts(u[r : r + 32, c : c + 256])
                act[r : r + 32, s + c : s + c + 256] = value.astype(BF16)
                slope[r : r + 32, s + c : s + c + 256] = deriv.astype(slope.dtype)


def feed_backward(product, slope, du, acc_bias):
    width = 512
    for s in range(0, slope.shape[1], width):
        dg = product(s, s + width).astype(F32)
        for c in range(0, width, 256):
            total = jnp.zeros((COLS, 256), F32)
            for r in range(0, CHUNK, 32):
                value = (
                    dg[r : r + 32, c : c + 256]
                    * slope[r : r + 32, s + c : s + c + 256].astype(F32)
                ).astype(BF16)
                du[r : r + 32, s + c : s + c + 256] = value
                total = total + column_sums(value.astype(F32), 32)
            acc_bias[:, s + c : s + c + 256] += total


def stretched(value):
    empty = jnp.zeros((COLS, value.shape[1]), F32)
    return jnp.concatenate([value, empty], axis=0).astype(BF16)


def by_head(value):
    return jnp.concatenate(
        [value * head_mask(value.shape[0], h, BF16) for h in range(LANES // HEAD_DIM)], axis=0
    )


def own_heads(product):
    size = COLS * COLS
    return sum(
        product[h * size : h * size + TOK, :] * head_mask(TOK, h, F32)
        for h in range(LANES // HEAD_DIM)
    )


def key_bias(where, window):
    size = COLS * COLS
    row = lax.broadcasted_iota(jnp.int32, (size, LANES), 0)
    high, wide = where.sides(window)
    inside = (row // COLS < high) & (row % COLS < wide)
    one = jnp.where(inside, 0.0, -MASK_FILL)
    return jnp.concatenate([one, one], axis=1)


def window_probs(keys, by_query, bias):
    scores = nt(keys, by_query) * HEAD_DIM ** (-0.5) + bias
    exponent = jnp.exp(scores - jnp.max(scores, axis=0, keepdims=True))
    return exponent * (1.0 / jnp.sum(exponent, axis=0, keepdims=True))


def window_rows(w):
    if isinstance(w, int):
        return slice(w * TOK, (w + 1) * TOK)
    return pl.ds(pl.multiple_of(w * TOK, COLS), TOK)


def spatial_forward(where, proj, dst, kept):
    width = dst.shape[1]

    def one(w):
        rows = window_rows(w)
        bias = key_bias(where, w)
        for k, s in enumerate(range(0, width, LANES)):
            query = stretched(proj[rows, s : s + LANES])
            keys = stretched(proj[rows, width + s : width + s + LANES])
            values = stretched(proj[rows, 2 * width + s : 2 * width + s + LANES])
            probs = window_probs(keys, by_head(query), bias)
            kept[w, k] = probs
            dst[rows, s : s + LANES] = own_heads(tn(probs.astype(BF16), values))

    for w in range(WPC):
        one(w)


def spatial_backward(kept, proj, upstream, dst):
    width = upstream.shape[1]
    scale = HEAD_DIM ** (-0.5)
    starts = range(0, width, LANES)
    for w in range(WPC):
        rows = window_rows(w)
        grads = [by_head(stretched(upstream[rows, s : s + LANES])) for s in starts]
        dprobs = []
        for s, grad in zip(starts, grads):
            values = stretched(proj[rows, 2 * width + s : 2 * width + s + LANES])
            dprobs.append(nt(values, grad))
        dots = [jnp.sum(kept[w, k] * v, axis=0, keepdims=True) for k, v in enumerate(dprobs)]
        dscores = [
            (kept[w, k] * (v - dot)).astype(BF16) for k, (v, dot) in enumerate(zip(dprobs, dots))
        ]
        for k, s in enumerate(starts):
            v_s = slice(2 * width + s, 2 * width + s + LANES)
            dst[rows, v_s] = nn(kept[w, k].astype(BF16), grads[k])[0:TOK]
        for k, s in enumerate(starts):
            query = by_head(stretched(proj[rows, s : s + LANES]))
            keys = stretched(proj[rows, width + s : width + s + LANES])
            dst[rows, s : s + LANES] = own_heads(tn(dscores[k], keys)) * scale
            k_s = slice(width + s, width + s + LANES)
            dst[rows, k_s] = nn(dscores[k], query)[0:TOK] * scale


def by_window(value):
    row = lax.broadcasted_iota(jnp.int32, value.shape, 0)
    return jnp.concatenate(
        [
            value * jnp.where((row >= w * TOK) & (row < (w + 1) * TOK), 1.0, 0.0).astype(BF16)
            for w in range(WPC)
        ],
        axis=1,
    )


def own_windows(product):
    return jnp.concatenate(
        [
            product[w * TOK : (w + 1) * TOK, w * LANES : (w + 1) * LANES] for w in range(WPC)
        ],
        axis=0,
    )


def gram_add(where, left, right, acc):
    images = [where.image(w, acc.shape[0]) for w in range(WPC)]
    for s in range(0, acc.shape[2], LANES):
        full = tn(left(s), by_window(right(s)))
        for w in range(WPC):
            part = sum(
                full[h * HEAD_DIM : (h + 1) * HEAD_DIM, w * LANES : (w + 1) * LANES]
                * head_mask(HEAD_DIM, h, F32)
                for h in range(LANES // HEAD_DIM)
            )
            acc[images[w], :, s : s + LANES] += part


def image_blocks(table, images, s, axis):
    return jnp.concatenate([head_blocks(table[i, :, s : s + LANES]) for i in images], axis=axis)


def gram_out(chunk, acc, mine, other):
    half = acc.shape[0] // 2

    @pl.when(chunk == pl.num_programs(0) - 1)
    def _():
        mine[...] = acc[0:half].reshape(mine.shape)
        other[...] = acc[half : 2 * half].reshape(other.shape)


def vector_out(chunk, acc, vec, bias_acc=None, bias=None):
    @pl.when(chunk == pl.num_programs(0) - 1)
    def _():
        vec[...] = jnp.sum(acc[...], axis=1)
        if bias is not None:
            bias[...] = jnp.sum(bias_acc[...], axis=0, keepdims=True)


def head_blocks(packed):
    return jnp.concatenate([packed] * (LANES // HEAD_DIM), axis=0) * block_mask(BF16)


def as_lines(value):
    return value.reshape(LINES, COLS, value.shape[1])


def spatial_kernel(
    globs, place, gi, li, ext,
    gx, lx, sk, sg, ss, ck, cg, cs, sb1, wqkv, wproj, w1, w2, wcqkv,
    c1_o, h1_o, p_o, o_o, c2_o, c3_o, h2_o, g_o, gp_o, mid_o, cc1_o, ch1_o, cp_o, probs_o,
    mine_o, other_o,
    wide, tok, valid, proj, att, gram, sv, cv,
):
    chunk = pl.program_id(0)
    width = gx.shape[3]
    where = Where(globs, chunk, place, gi, li, ext)
    gate = where.gate

    @pl.when(chunk == 0)
    def _():
        gram[...] = jnp.zeros_like(gram)
        wide[:, 14:16, :] = jnp.zeros((14, 2, width), F32)
        fill_vec(sk, sg, ss, sv)
        fill_vec(ck, cg, cs, cv)

    fill_valid(where, valid)
    load_tokens(chunk, globs, gx, lx, tok, wide)
    conv_forward(tok, valid, sv, 0, 20, gate, c1_o)
    norm_forward(c1_o, sv, 18, 22, h1_o)
    for j in range(3):
        cols = slice(j * width, (j + 1) * width)
        part = nn(h1_o[...], wqkv[:, cols])
        if j != 1:
            row = 24 if j == 0 else 25
            part = part + sv[row : row + 1, :]
        part = part.astype(BF16)
        p_o[:, cols] = part
        proj[:, cols] = part.astype(F32)
    spatial_forward(where, proj, att, probs_o)
    o_o[...] = att[...].astype(BF16)
    c2_o[...] = c1_o[...] + as_lines(nn(o_o[...], wproj[...]) + sv[26:27, :])
    conv_forward(c2_o, valid, sv, 9, 21, gate, c3_o)
    norm_forward(c3_o, sv, 19, 23, h2_o)
    feed_forward(h2_o, w1, sb1, g_o, gp_o)
    mid_o[...] = c3_o[...] + as_lines(nn(g_o[...], w2[...]) + sv[27:28, :])
    conv_forward(mid_o, valid, cv, 0, 20, gate, cc1_o)
    norm_forward(cc1_o, cv, 18, 22, ch1_o)
    for j in range(3):
        cols = slice(j * width, (j + 1) * width)
        part = nn(ch1_o[...], wcqkv[:, cols]) + cv[24 + j : 25 + j, :]
        if j == 0:
            mask = jnp.concatenate([valid[...].reshape(CHUNK, LANES)] * (width // LANES), axis=1)
            part = part * mask
        cp_o[:, cols] = part.astype(BF16)
    gram_add(
        where,
        lambda s: cp_o[:, width + s : width + s + LANES],
        lambda s: cp_o[:, s : s + LANES],
        gram,
    )
    gram_out(chunk, gram, mine_o, other_o)


def channel_kernel(
    globs, place, gi, li, ext,
    a_all, cc1, cvals, dout, dg, vec_i, ck, cg, cs, cb1, wproj, w1, w1_t, w2,
    gout, lout, o_o, h2_o, g_o, du_o, dc2_o, dob_o, do_o, mine_o, other_o, vec_o, bias_o,
    wide, tok, valid, c2_s, c3_s, slope, dhid, dgram, vg, vb, cv,
):
    chunk = pl.program_id(0)
    width = cc1.shape[2]
    where = Where(globs, chunk, place, gi, li, ext)
    gate = where.gate

    @pl.when(chunk == 0)
    def _():
        dgram[...] = jnp.zeros_like(dgram)
        vg[...] = jnp.zeros_like(vg)
        vb[...] = jnp.zeros_like(vb)
        wide[:, 14:16, :] = jnp.zeros((14, 2, width), F32)
        fill_vec(ck, cg, cs, cv)
        vg[:, 0, :] = vec_i[...]

    fill_valid(where, valid)
    images = [where.image(w, a_all.shape[0]) for w in range(WPC)]
    for s in range(0, width, LANES):
        product = nn(cvals[:, s : s + LANES], image_blocks(a_all, images, s, 1))
        o_o[:, s : s + LANES] = own_windows(product).astype(BF16)
    c2_s[...] = cc1[...] + as_lines(nn(o_o[...], wproj[...]) + cv[27:28, :])
    conv_forward(c2_s, valid, cv, 9, 21, gate, c3_s)
    norm_forward(c3_s, cv, 19, 23, h2_o)
    feed_forward(h2_o, w1, cb1, g_o, slope)
    tok[...] = c3_s[...] + as_lines(nn(g_o[...], w2[...]) + cv[28:29, :])
    store_tokens(chunk, globs, tok, gout, lout, wide)

    tok[...] = as_lines(dout[...].astype(F32))
    feed_backward(lambda s, e: dg[:, s:e], slope, du_o, vb)
    dhid[...] = nn(du_o[...], w1_t[...])
    norm_backward(dhid, c3_s, cv, 19, tok, tok, vg, 10, 11)
    conv_backward(tok, c2_s, valid, cv, 9, gate, dc2_o, vg, 0, 9)
    low = dc2_o[...].reshape(CHUNK, width).astype(BF16)
    dob_o[...] = low
    vg[12] += column_sums(low.astype(F32))
    do_o[...] = nt(dob_o[...], wproj[...]).astype(BF16)
    gram_add(
        where,
        lambda s: cvals[:, s : s + LANES],
        lambda s: do_o[:, s : s + LANES],
        dgram,
    )
    gram_out(chunk, dgram, mine_o, other_o)
    vector_out(chunk, vg, vec_o, vb, bias_o)


def channel_back_kernel(
    globs, place, gi, li, ext,
    a_all, ds_all, cp, do, dc2, cc1, mid, ck, cg, cs, wqkv,
    dp_o, dmid_o, vec_o,
    tok, valid, dhid, vg, cv,
):
    chunk = pl.program_id(0)
    width = do.shape[1]
    where = Where(globs, chunk, place, gi, li, ext)
    gate = where.gate

    @pl.when(chunk == 0)
    def _():
        vg[...] = jnp.zeros_like(vg)
        fill_vec(ck, cg, cs, cv)

    fill_valid(where, valid)
    scale = channel_scale()
    images = [where.image(w, a_all.shape[0]) for w in range(WPC)]
    mask = valid[...].reshape(CHUNK, LANES)
    for s in range(0, width, LANES):
        q_s, k_s, v_s = [slice(j * width + s, j * width + s + LANES) for j in range(3)]
        blocks = image_blocks(ds_all, images, s, 1)
        low = (own_windows(nn(cp[:, k_s], blocks)) * (scale * mask)).astype(BF16)
        dp_o[:, q_s] = low
        vg[12, :, s : s + LANES] += column_sums(low.astype(F32))
        blocks = image_blocks(ds_all, images, s, 0)
        low = (own_windows(nt(cp[:, q_s], blocks)) * scale).astype(BF16)
        dp_o[:, k_s] = low
        vg[13, :, s : s + LANES] += column_sums(low.astype(F32))
        blocks = image_blocks(a_all, images, s, 0)
        low = own_windows(nt(do[:, s : s + LANES], blocks)).astype(BF16)
        dp_o[:, v_s] = low
        vg[14, :, s : s + LANES] += column_sums(low.astype(F32))
    dhid[...] = nt(dp_o[...], wqkv[...])
    norm_backward(dhid, cc1, cv, 18, dc2, tok, vg, 10, 11)
    conv_backward(tok, mid, valid, cv, 0, gate, dmid_o, vg, 0, 9)
    vector_out(chunk, vg, vec_o)


def cot_kernel(globs, place, gcot, lcot, w2, dout_o, dg_o, vec_o, wide, tok, vg):
    chunk = pl.program_id(0)
    width = gcot.shape[3]

    @pl.when(chunk == 0)
    def _():
        vg[...] = jnp.zeros_like(vg)
        wide[:, 14:16, :] = jnp.zeros((14, 2, width), F32)

    load_tokens(chunk, globs, gcot, lcot, tok, wide)
    flat = tok[...].reshape(CHUNK, width)
    vg[13] += column_sums(flat)
    dout_o[...] = flat.astype(BF16)
    for s in range(0, w2.shape[0], 512):
        dg_o[:, s : s + 512] = nt(dout_o[...], w2[s : s + 512, :]).astype(BF16)
    vector_out(chunk, vg, vec_o)


def turn_kernel(*refs):
    half = len(refs) // 2
    for src, dst in zip(refs[:half], refs[half:]):
        dst[...] = jnp.transpose(src[...])


def turned_weights(*weights):
    steps = 4

    def spec(shape, step_dim):
        block = tuple(n // steps if d == step_dim else n for d, n in enumerate(shape))
        return pl.BlockSpec(block, lambda j: (j, 0) if step_dim == 0 else (0, j))

    longs = [0 if w.shape[0] > w.shape[1] else 1 for w in weights]
    return pl.pallas_call(
        turn_kernel,
        grid=(steps,),
        in_specs=[spec(w.shape, d) for w, d in zip(weights, longs)],
        out_specs=[spec(w.shape[::-1], 1 - d) for w, d in zip(weights, longs)],
        out_shape=[jax.ShapeDtypeStruct(w.shape[::-1], BF16) for w in weights],
        compiler_params=pltpu.CompilerParams(
            dimension_semantics=("arbitrary",), vmem_limit_bytes=VMEM
        ),
        name="turned_weights",
    )(*weights)


def hidden_back_kernel(
    globs, place, gi, li, ext,
    c2, c3, gp, dmid, sk, sg, ss, wproj, w1_t, w2_t,
    du_o, dmb_o, dob_o, dc2_o, do_o, vec_o, bias_o,
    tok, valid, dhid, vg, vb, sv,
):
    chunk = pl.program_id(0)
    width = wproj.shape[0]
    where = Where(globs, chunk, place, gi, li, ext)

    @pl.when(chunk == 0)
    def _():
        vg[...] = jnp.zeros_like(vg)
        vb[...] = jnp.zeros_like(vb)
        fill_vec(sk, sg, ss, sv)

    fill_valid(where, valid)
    low = dmid[...].reshape(CHUNK, width).astype(BF16)
    dmb_o[...] = low
    vg[13] += column_sums(low.astype(F32))
    upstream = dmb_o[...]
    feed_backward(lambda s, e: nn(upstream, w2_t[:, s:e]), gp, du_o, vb)
    dhid[...] = nn(du_o[...], w1_t[...])
    norm_backward(dhid, c3, sv, 19, dmid, tok, vg, 10, 11)
    conv_backward(tok, c2, valid, sv, 9, where.gate, dc2_o, vg, 0, 9)
    low = dc2_o[...].reshape(CHUNK, width).astype(BF16)
    dob_o[...] = low
    vg[12] += column_sums(low.astype(F32))
    do_o[...] = nt(dob_o[...], wproj[...]).astype(BF16)
    vector_out(chunk, vg, vec_o, vb, bias_o)


def window_back_kernel(probs, p, do, *refs):
    dp_o, vec_o, proj, att, dproj, vg = refs[-6:]
    chunk = pl.program_id(0)
    width = do.shape[1]

    @pl.when(chunk == 0)
    def _():
        vg[...] = jnp.zeros_like(vg)
        if len(refs) > 6:
            vg[:, 0, :] = refs[0][...]

    att[...] = do[...].astype(F32)
    proj[...] = p[...].astype(F32)
    spatial_backward(probs, proj, att, dproj)
    for j in range(3):
        low = dproj[:, j * width : (j + 1) * width].astype(BF16)
        dp_o[:, j * width : (j + 1) * width] = low
        vg[12 + j] += column_sums(low.astype(F32))
    vector_out(chunk, vg, vec_o)


def window_back(probs, p, do, first, count, base):
    width = do.shape[1]
    specs = [
        pl.BlockSpec((WPC,) + probs.shape[1:], lambda i: (i + first, 0, 0, 0)),
        pl.BlockSpec((CHUNK, 3 * width), lambda i: (i + first, 0)),
        pl.BlockSpec((CHUNK, width), lambda i: (i + first, 0)),
    ]
    args, aliases = [probs, p, do], {}
    if base is not None:
        args += [base[1], base[0]]
        specs += [keep((16, width)), pl.BlockSpec(memory_space=pl.ANY)]
        aliases = {4: 0}
    return pl.pallas_call(
        window_back_kernel,
        grid=(count,),
        in_specs=specs,
        out_specs=[
            pl.BlockSpec((CHUNK, 3 * width), lambda i: (i + first, 0)),
            keep((16, width)),
        ],
        out_shape=[
            jax.ShapeDtypeStruct(p.shape, BF16),
            jax.ShapeDtypeStruct((16, width), F32),
        ],
        scratch_shapes=[
            pltpu.VMEM((CHUNK, 3 * width), F32),
            pltpu.VMEM((CHUNK, width), F32),
            pltpu.VMEM((CHUNK, 3 * width), F32),
            pltpu.VMEM((16, COLS, width), F32),
        ],
        input_output_aliases=aliases,
        compiler_params=pltpu.CompilerParams(
            dimension_semantics=("arbitrary",), vmem_limit_bytes=VMEM
        ),
        cost_estimate=pl.CostEstimate(
            flops=16 * count * CHUNK * 256 * width,
            bytes_accessed=count * (16 * CHUNK * width + 4 * probs[0].size * WPC),
            transcendentals=0,
        ),
        name="window_back",
    )(*args)


def first_back_kernel(
    globs, place, gi, li, ext,
    gx, lx, c1, dp, dc2, sk, sg, ss, wqkv, vec_i,
    gg, lg, vec_o,
    wide, tok, tok2, valid, dhid, vg, sv,
):
    chunk = pl.program_id(0)
    width = gx.shape[3]
    where = Where(globs, chunk, place, gi, li, ext)

    @pl.when(chunk == 0)
    def _():
        vg[...] = jnp.zeros_like(vg)
        vg[:, 0, :] = vec_i[...]
        wide[:, 14:16, :] = jnp.zeros((14, 2, width), F32)
        fill_vec(sk, sg, ss, sv)

    fill_valid(where, valid)
    dhid[...] = nt(dp[...], wqkv[...])
    norm_backward(dhid, c1, sv, 18, dc2, tok2, vg, 10, 11)
    load_tokens(chunk, globs, gx, lx, tok, wide)
    lines_ref = dhid.reshape(LINES, COLS, width)
    conv_backward(tok2, tok, valid, sv, 0, where.gate, lines_ref, vg, 0, 9)
    store_tokens(chunk, globs, lines_ref, gg, lg, wide)
    vector_out(chunk, vg, vec_o)


def weight_kernel(y, x, out):
    out[...] = tn(y[...], x[...]).astype(BF16).reshape(out.shape)


def group_kernel(kinds, counts, mode, skip, place, *refs):
    ins = sum(counts)
    outs = 1 if mode == "one" else 2
    static = mode != "xor"
    buffers, product = refs[ins + skip : ins + skip + outs], refs[ins + skip + outs]
    turned = list(refs[ins + skip + outs + 1 :])
    shape = buffers[0].shape
    parts, lines_of, lanes = shape[-4], shape[-3], shape[-1]
    core, line, quarter = (0, 0, 0) if static else (place[0], place[1], place[2])
    step = pl.program_id(0)

    def put(q, j, at, values, lane=0):
        rows = slice(at, at + values[0].shape[0])
        cols = slice(lane, lane + values[0].shape[1])
        if mode == "pair":
            swap = place[0] == 1
            values = [jnp.where(swap, values[1 - rel], values[rel]) for rel in range(2)]
            q = jnp.bitwise_xor(place[2], q)
        for rel in range(2):
            value = values[rel].astype(BF16)
            if mode == "one":
                buffers[0][rel, q, j, rows, cols] = value
            else:
                buffers[rel][q, j, rows, cols] = value

    def rows_at(start, size):
        if isinstance(start, int):
            return slice(start, start + size)
        return pl.ds(pl.multiple_of(start, 16), size)

    at, first = 0, 0
    for kind, count in zip(kinds, counts):
        args = refs[first : first + count]
        first += count
        if kind == "vec":
            *vecs, bias_a, bias_b = args
            col = vecs[0].shape[1] // (2 * lines_of)
            size = bias_a.shape[1] // (2 * lines_of)

            @pl.when(step == 0)
            def _(vecs=vecs, bias_a=bias_a, bias_b=bias_b, at=at, col=col, size=size):
                cuts = [slice(k * col, (k + 1) * col) for k in range(2 * lines_of)]
                wide = [slice(k * size, (k + 1) * size) for k in range(2 * lines_of)]
                fill = jnp.zeros((14, size), F32)
                for j in range(lines_of):
                    for q, vec in enumerate(vecs):
                        put(q, j, at, [vec[:, cuts[2 * j + rel]] for rel in range(2)])
                    last = [
                        jnp.concatenate(
                            [bias_a[:, wide[2 * j + rel]], bias_b[:, wide[2 * j + rel]], fill],
                            axis=0,
                        )
                        for rel in range(2)
                    ]
                    put(parts - 1, j, at, last)

            at += 16
        elif kind == "side":
            y, x = args
            x_t = turned.pop(0)

            @pl.when(step == 0)
            def _(x=x, x_t=x_t):
                x_t[...] = jnp.transpose(x[...])

            size = y.shape[1] // 2
            halves = [nn(x_t[...], y[:, rel * size : (rel + 1) * size]) for rel in range(2)]
            each = size // parts
            for q in range(parts):
                for half in range(lanes // size):
                    start = (q * (lanes // size) + half) * each
                    values = [halves[rel][start : start + each, :] for rel in range(2)]
                    put(q, step, at, values, half * size)
            at += each
        else:
            y, x = args
            n = y.shape[1]
            if kind == "rows":
                y_t = turned.pop(0)

                @pl.when(step == 0)
                def _(y=y, y_t=y_t):
                    y_t[...] = jnp.transpose(y[...])

                result = nn(y_t[...], x[...])
                each = n // (2 * lines_of)
            else:
                result = tn(y[...], x[...])
                each = n // (2 * parts)
            if not static:
                product[0:n, :] = result
                result = product
            for e in range(lines_of if kind == "rows" else parts):
                values = []
                for rel in range(2):
                    side = core ^ rel if static else jnp.bitwise_xor(core, rel)
                    mine = line if kind == "rows" else quarter
                    own = mine ^ e if static else jnp.bitwise_xor(mine, e)
                    if kind == "rows":
                        start = (own * 2 + side) * each
                    else:
                        start = (side * parts + own) * each
                    values.append(result[rows_at(start, each), :])
                if kind == "rows":
                    put(step, e, at, values)
                else:
                    put(e, step, at, values)
            at += each


def group_grad(
    place, groups, kinds, mode, lanes, lines_of, parts, name, blocks=(0, 1), base=None, hint=1
):
    total = groups[0][0].shape[0]
    specs, args, rows, flops, turned = [], [], 0, 0, []

    def moving(size, which):
        if mode != "xor":
            return pl.BlockSpec((total, size), lambda j, at: (0, j))
        return pl.BlockSpec((total, size), lambda j, at: (0, jnp.bitwise_xor(at[which], j)))

    for operands, kind in zip(groups, kinds):
        args += operands
        if kind == "vec":
            specs += [keep(v.shape) for v in operands]
            rows += 16
            continue
        y, x = operands
        n, m = y.shape[1], x.shape[1]
        flops += 2 * total * n * m
        if kind == "rows":
            specs += [hold((total, n)), moving(m // parts, 2)]
            turned.append(pltpu.VMEM((n, total), BF16))
            rows += n // (2 * lines_of)
        else:
            specs += [moving(n // lines_of, 1), hold((total, m))]
            if kind == "side":
                turned.append(pltpu.VMEM((m, total), BF16))
            rows += n * m // (2 * lines_of * parts * lanes)
    block, count = blocks
    if mode == "one":
        outs = [jax.ShapeDtypeStruct((2, parts, lines_of, count * rows, lanes), BF16)]
        out_specs = [
            pl.BlockSpec((2, parts, lines_of, rows, lanes), lambda j, at: (0, 0, 0, block, 0))
        ]
    else:
        outs = [jax.ShapeDtypeStruct((parts, lines_of, rows, lanes), BF16)] * 2
        out_specs = [keep(o.shape) for o in outs]
    aliases = {}
    if base is not None:
        aliases = {1 + len(args): 0}
        args.append(base)
        specs.append(pl.BlockSpec(memory_space=pl.ANY))
    size = sum(a.size * a.dtype.itemsize for a in args) + 4 * parts * lines_of * rows * lanes
    counts = [len(g) for g in groups]
    return pl.pallas_call(
        functools.partial(group_kernel, kinds, counts, mode, 0 if base is None else 1),
        grid_spec=pltpu.PrefetchScalarGridSpec(
            num_scalar_prefetch=1,
            grid=(parts,),
            in_specs=specs,
            out_specs=out_specs,
            scratch_shapes=[pltpu.VMEM((512, lanes), F32)] + turned,
        ),
        out_shape=outs,
        input_output_aliases=aliases,
        compiler_params=pltpu.CompilerParams(
            dimension_semantics=("arbitrary",), vmem_limit_bytes=VMEM
        ),
        cost_estimate=pl.CostEstimate(
            flops=hint * flops, bytes_accessed=hint * size, transcendentals=0
        ),
        name=name,
    )(place, *args)


def sum_kernel(count, *refs):
    ins, outs = refs[:count], refs[count:]
    for d, dst in enumerate(outs):
        total = ins[0][d].astype(F32)
        for src in ins[1:]:
            total = total + src[d].astype(F32)
        dst[...] = total.astype(dst.dtype)


def sum_split(arrays, name):
    n, rows, lanes = arrays[0].shape
    steps = 4 if rows >= 512 else 1
    kind = jax.ShapeDtypeStruct((rows, lanes), arrays[0].dtype)
    return pl.pallas_call(
        functools.partial(sum_kernel, len(arrays)),
        grid=(steps,),
        in_specs=[pl.BlockSpec((n, rows // steps, lanes), lambda j: (0, j, 0))] * len(arrays),
        out_specs=[pl.BlockSpec((rows // steps, lanes), lambda j: (j, 0))] * n,
        out_shape=[kind] * n,
        compiler_params=pltpu.CompilerParams(
            dimension_semantics=("arbitrary",), vmem_limit_bytes=VMEM
        ),
        cost_estimate=pl.CostEstimate(flops=0, bytes_accessed=0, transcendentals=0),
        name=name,
    )(*arrays)


def small_call(body, grid, args, in_specs, outs, out_specs, name):
    return pl.pallas_call(
        body,
        grid=grid,
        in_specs=in_specs,
        out_specs=out_specs,
        out_shape=outs,
        compiler_params=pltpu.CompilerParams(
            dimension_semantics=("arbitrary",), vmem_limit_bytes=VMEM
        ),
        cost_estimate=pl.CostEstimate(flops=0, bytes_accessed=0, transcendentals=0),
        name=name,
    )(*args)


def added(*refs):
    return sum(r[...].astype(F32) for r in refs)


def halved_core(mine, got):
    parts, lines_of, rows, lanes = mine.shape
    half = rows // 2
    spec = pl.BlockSpec((parts, 1, rows, lanes), lambda j: (0, j, 0, 0))
    out = jax.ShapeDtypeStruct((2, lines_of, half, lanes), BF16)
    out_spec = pl.BlockSpec((2, 1, half, lanes), lambda j: (0, j, 0, 0))
    plans = [(0, (0, 2)), (0, (1, 3)), (1, (0, 1)), (1, (2, 3))]

    def body(a, b, *outs):
        total = added(a, b).astype(BF16)
        for dst, (part, chosen) in zip(outs, plans):
            for k, q in enumerate(chosen):
                dst[k, 0] = total[q, 0, part * half : (part + 1) * half]

    return small_call(
        body, (lines_of,), (mine, got), [spec] * 2, [out] * 4, [out_spec] * 4, "s_sum_core"
    )


def halved_first(a, ra, b, rb):
    _, lines_of, half, lanes = a.shape
    spec = pl.BlockSpec((2, 1, half, lanes), lambda j: (0, j, 0, 0))
    out = jax.ShapeDtypeStruct((lines_of, half, lanes), BF16)
    out_spec = pl.BlockSpec((1, half, lanes), lambda j: (j, 0, 0))

    def body(a, ra, b, rb, a0, a1, b0, b1):
        first, second = added(a, ra).astype(BF16), added(b, rb).astype(BF16)
        a0[...], a1[...] = first[0], first[1]
        b0[...], b1[...] = second[0], second[1]

    return small_call(
        body, (lines_of,), (a, ra, b, rb), [spec] * 4, [out] * 4, [out_spec] * 4, "s_sum_first"
    )


def halved_second(a, ra, b, rb):
    lines_of, half, lanes = a.shape
    spec = pl.BlockSpec((1, half, lanes), lambda j: (j, 0, 0))
    out = jax.ShapeDtypeStruct((lines_of, 2 * half, lanes), BF16)
    out_spec = pl.BlockSpec((1, 2 * half, lanes), lambda j: (j, 0, 0))

    def body(a, ra, b, rb, dst):
        dst[:, 0:half] = added(a, ra).astype(BF16)
        dst[:, half : 2 * half] = added(b, rb).astype(BF16)

    return small_call(
        body, (lines_of,), (a, ra, b, rb), [spec] * 4, out, out_spec, "s_sum_second"
    )


def sum_with_vectors(arrays, vectors, name):
    lines_of, rows, lanes = arrays[0].shape
    extra = vectors[0].shape[0]
    out = jax.ShapeDtypeStruct((rows + extra, lanes), BF16)

    def body(*refs):
        ins, vecs = refs[: len(arrays)], refs[len(arrays) : len(arrays) + len(vectors)]
        total, vector = added(*ins).astype(BF16), added(*vecs).astype(BF16)
        for j, dst in enumerate(refs[len(arrays) + len(vectors) :]):
            dst[0:rows] = total[j]
            dst[rows : rows + extra] = vector

    return small_call(
        body, (1,), (*arrays, *vectors), [keep(v.shape) for v in (*arrays, *vectors)],
        [out] * lines_of, [keep(out.shape)] * lines_of, name,
    )


def exchange(array, axis, flip=1):
    size = lax.axis_size(axis)
    return lax.ppermute(array, axis, [(i, i ^ flip) for i in range(size)])


def group_sum_core(mine, other, name):
    parts, lines_of, rows, lanes = mine.shape
    flat = (parts, lines_of * rows, lanes)
    got = exchange(other, "core")
    return sum_split([mine.reshape(flat), got.reshape(flat)], name + "_sum_core")


def group_sum_line(pieces, name):
    held = [pieces[0]] + [exchange(pieces[d], "line", d) for d in range(1, len(pieces))]
    return sum_split([v[None] for v in held], name + "_sum_line")[0]


def quarters(mine):
    return [mine] + [exchange(mine, "img", d) for d in range(1, lax.axis_size("img"))]


def unpack_kernel(groups, place, *refs):
    ins = sum(parts for parts, _ in groups)
    pieces, outs, fulls = list(refs[:ins]), list(refs[ins : -len(groups)]), refs[-len(groups) :]
    vecs = []
    for (parts, kinds), full in zip(groups, fulls):
        for d in range(parts):
            full[jnp.bitwise_xor(place[2], d)] = pieces.pop(0)[...].astype(F32)
        at, lanes = 0, full.shape[2]
        for kind in kinds:
            if kind in ("vec", "late"):
                vecs.append((full, at))
                at += 16
                continue
            dst = outs.pop(0)
            if kind == "rows":
                rows = dst.shape[0]
                for q in range(parts):
                    dst[:, q * lanes : (q + 1) * lanes] = full[q, at : at + rows, :]
                at += rows
            elif kind == "side":
                size = dst.shape[1]
                each = size // parts
                for q in range(parts):
                    for half in range(lanes // size):
                        start = (q * (lanes // size) + half) * each
                        dst[start : start + each, :] = full[
                            q, at : at + each, half * size : (half + 1) * size
                        ]
                at += each
            else:
                rows = dst.shape[0]
                each = rows // parts
                dst[...] = full[:, at : at + each, :].reshape(rows, lanes)
                at += each
    (full_b, at_b), (full_c, at_c) = vecs
    col = outs[0].shape[2]
    me = place[1] * 2 + place[0]

    def small(first, second, attn, kernels, gains, shifts):
        for t in range(9):
            kernels[t, 0:1, :] = first[t : t + 1]
            kernels[t, 1:2, :] = second[t : t + 1]
        gains[0:1, :] = first[10:11]
        gains[1:2, :] = second[10:11]
        rows = [first[9:10], second[9:10], first[11:12], second[11:12]]
        rows += [first[r : r + 1] for r in attn] + [second[12:13], second[13:14]]
        for r, row in enumerate(rows):
            shifts[r : r + 1, :] = row

    c2, c1, s2, bias = [full_b[q, at_b : at_b + 16, :] for q in range(4)]
    rows = [full_c[q, at_c : at_c + 16, :] for q in range(full_c.shape[0])]
    while len(rows) > 1:
        rows = [a + b for a, b in zip(rows[0::2], rows[1::2])]
    s1 = pltpu.roll(rows[0], rows[0].shape[1] - me * col, 1)
    small(s1[:, 0:col], s2[:, 0:col], (12, 14), *outs[0:3])
    small(c1[:, 0:col], c2[:, 0:col], (12, 13, 14), *outs[4:7])
    share = outs[3].shape[1]
    outs[3][...] = bias[1:2, 0:share]
    outs[7][...] = bias[0:1, 0:share]


def group_unpack(place, groups, outs, name):
    pieces = [p for held, _ in groups for p in held]
    return pl.pallas_call(
        functools.partial(unpack_kernel, [(len(held), kinds) for held, kinds in groups]),
        grid_spec=pltpu.PrefetchScalarGridSpec(
            num_scalar_prefetch=1,
            grid=(1,),
            in_specs=[keep(p.shape) for p in pieces],
            out_specs=[keep(o) for o in outs],
            scratch_shapes=[
                pltpu.VMEM((len(held),) + held[0].shape, F32) for held, _ in groups
            ],
        ),
        out_shape=[jax.ShapeDtypeStruct(o, F32) for o in outs],
        compiler_params=pltpu.CompilerParams(
            dimension_semantics=("arbitrary",), vmem_limit_bytes=VMEM
        ),
        name=name,
    )(place, *pieces)


def together(*values):
    return lax.optimization_barrier(values)


def after(value, *others):
    return lax.optimization_barrier((value,) + others)[0]


def all_sum(small):
    for axis in ("core", "line", "img"):
        held = [small] + [exchange(small, axis, d) for d in range(1, lax.axis_size(axis))]
        while len(held) > 1:
            held = [a + b for a, b in zip(held[0::2], held[1::2])]
        small = held[0]
    return small


def image_sum(mine, other, beside=None):
    mine = mine + exchange(other, "core")
    held = [exchange(mine[d], "line", d) for d in range(1, mine.shape[0])]
    extra = None
    if beside is not None:
        extra = beside(mine)
        held = lax.optimization_barrier((held, extra))[0]
    return mine[0] + sum(held), extra


def image_gather(mine, lines_of, beside=None):
    held = [exchange(mine, "line", d) for d in range(1, lines_of)]
    extra = None
    if beside is not None:
        extra = beside(mine)
        held = lax.optimization_barrier((held, extra))[0]
    held = jnp.stack([mine] + held)
    return jnp.concatenate([held, exchange(held, "core")], axis=0), extra


def hold(shape):
    return pl.BlockSpec(
        shape, lambda i, *_: (0,) * len(shape), pipeline_mode=pl.Buffered(1)
    )


def keep(shape):
    return pl.BlockSpec(shape, lambda i, *_: (0,) * len(shape))


def lines(width):
    return pl.BlockSpec((LINES, COLS, width), lambda i, *_: (i, 0, 0))


def tokens(width, col=0):
    return pl.BlockSpec((CHUNK, width), lambda i, *_: (i, col))


def call(body, chunks, prefetch, args, in_specs, outs, out_specs, scratch, flops, name):
    size = sum(a.size * a.dtype.itemsize for a in args) + sum(
        functools.reduce(lambda a, b: a * b, o.shape) * o.dtype.itemsize for o in outs
    )
    return pl.pallas_call(
        body,
        grid_spec=pltpu.PrefetchScalarGridSpec(
            num_scalar_prefetch=len(prefetch),
            grid=(chunks,),
            in_specs=in_specs,
            out_specs=out_specs,
            scratch_shapes=scratch,
        ),
        out_shape=outs,
        compiler_params=pltpu.CompilerParams(
            dimension_semantics=("arbitrary",), vmem_limit_bytes=VMEM
        ),
        cost_estimate=pl.CostEstimate(flops=flops, bytes_accessed=size, transcendentals=0),
        name=name,
    )(*prefetch, *args)


def weight_grad(y, x, name):
    total, n = y.shape
    m = x.shape[1]
    step = 256
    return pl.pallas_call(
        weight_kernel,
        grid=(n // step,),
        in_specs=[pl.BlockSpec((total, step), lambda j: (0, j)), hold((total, m))],
        out_specs=pl.BlockSpec((step, m), lambda j: (j, 0)),
        out_shape=jax.ShapeDtypeStruct((n, m), BF16),
        compiler_params=pltpu.CompilerParams(
            dimension_semantics=("arbitrary",), vmem_limit_bytes=VMEM
        ),
        cost_estimate=pl.CostEstimate(
            flops=2 * total * n * m,
            bytes_accessed=2 * (total * (n + m) + n * m),
            transcendentals=0,
        ),
        name=name,
    )(y, x)


def shards(
    glob_x, loc_x, glob_cot, loc_cot, loc_extent, glob_image, loc_image,
    s_kernels, s_gains, s_shifts, s_qkv, s_proj, s_fc1, s_fc1_bias, s_fc2,
    c_kernels, c_gains, c_shifts, c_qkv, c_proj, c_fc1, c_fc1_bias, c_fc2,
):
    globs, locs = glob_x.shape[0], loc_x.shape[0]
    width = glob_x.shape[3]
    hidden = s_fc1.shape[1]
    chunks = globs + locs // WPC
    total = chunks * CHUNK
    parts, lines_of = lax.axis_size("img"), lax.axis_size("line")
    groups = 2 * lines_of
    images = glob_image.shape[0] // 2
    per = images // groups
    core, line = lax.axis_index("core"), lax.axis_index("line")
    me = 2 * line + core
    place = jnp.stack([core, line, lax.axis_index("img"), jnp.int32(lines_of)])
    scalars = (place, glob_image, loc_image, loc_extent.T)
    s_vecs = (s_kernels.transpose(1, 0, 2), s_gains, s_shifts)
    c_vecs = (c_kernels.transpose(1, 0, 2), c_gains, c_shifts)

    def f3(w=width):
        return jax.ShapeDtypeStruct((total // COLS, COLS, w), F32)

    def b2(w=width):
        return jax.ShapeDtypeStruct((total, w), BF16)

    def sh(*shape):
        return jax.ShapeDtypeStruct(shape, F32)

    glob_spec = pl.BlockSpec(
        (1, 14, 14, width), lambda i, *_: (jnp.minimum(i, globs - 1), 0, 0, 0)
    )
    loc_spec = pl.BlockSpec(
        (WPC, WIN, WIN, width), lambda i, *_: (jnp.maximum(i - globs, 0), 0, 0, 0)
    )
    s_wide = pltpu.VMEM((14, 16, width), F32)
    s_tok = pltpu.VMEM((LINES, COLS, width), F32)
    s_valid = pltpu.VMEM((LINES, COLS, LANES), F32)
    s_vec = pltpu.VMEM((32, width), F32)
    s_gram = pltpu.VMEM((images, HEAD_DIM, width), F32)
    s_acc = pltpu.VMEM((16, COLS, width), F32)
    s_bias = pltpu.VMEM((COLS, hidden), F32)

    def s_flat(w):
        return pltpu.VMEM((CHUNK, w), F32)

    s_specs, c_specs = [hold(v.shape) for v in s_vecs], [hold(v.shape) for v in c_vecs]
    half_sums = sh(lines_of, per * HEAD_DIM, width)
    gram_spec = hold((images, HEAD_DIM, width))
    w_qkv, w_proj = hold((width, 3 * width)), hold((width, width))
    w_fc1, w_fc2 = hold((width, hidden)), hold((hidden, width))
    dense = 2 * total * width * (4 * width + 2 * hidden)
    probs_shape = (chunks * WPC, width // LANES, COLS * COLS, 2 * LANES)
    probs_spec = pl.BlockSpec((WPC,) + probs_shape[1:], lambda i, *_: (i, 0, 0, 0))

    (c1, h1, p, o, c2, c3, h2, g, gp, mid, cc1, ch1, cp, probs_s, gram_a, gram_b) = call(
        functools.partial(spatial_kernel, globs), chunks, scalars,
        (glob_x, loc_x, *s_vecs, *c_vecs, s_fc1_bias.reshape(1, -1), s_qkv, s_proj, s_fc1, s_fc2,
         c_qkv),
        [glob_spec, loc_spec, *s_specs, *c_specs, hold((1, hidden)), w_qkv, w_proj, w_fc1, w_fc2,
         w_qkv],
        [f3(), b2(), b2(3 * width), b2(), f3(), f3(), b2(), b2(hidden), b2(hidden), f3(), f3(),
         b2(), b2(3 * width), sh(*probs_shape), half_sums, half_sums],
        [lines(width), tokens(width), tokens(3 * width), tokens(width), lines(width),
         lines(width), tokens(width), tokens(hidden), tokens(hidden), lines(width), lines(width),
         tokens(width), tokens(3 * width), probs_spec, keep(half_sums.shape),
         keep(half_sums.shape)],
        [s_wide, s_tok, s_valid, s_flat(3 * width), s_flat(width), s_gram, s_vec, s_vec],
        dense + 6 * total * width * width, "spatial_fwd",
    )

    def beside_cot(ready):
        return call(
            functools.partial(cot_kernel, globs), chunks, scalars[:1],
            (after(glob_cot, ready), loc_cot, c_fc2),
            [glob_spec, loc_spec, w_fc2],
            [b2(), b2(hidden), sh(16, width)],
            [tokens(width), tokens(hidden), keep((16, width))],
            [s_wide, s_tok, s_acc],
            2 * total * width * hidden, "channel_cot",
        )

    def beside_turn(ready):
        return turned_weights(s_fc1, s_fc2, after(c_fc1, ready))

    scores, (dout, cdg, cvec0) = image_sum(gram_a, gram_b, beside_cot)
    scores = scores.reshape(per, HEAD_DIM, width) * channel_scale()
    exponent = jnp.exp(scores - jnp.max(scores, axis=1, keepdims=True))
    probs = exponent / jnp.sum(exponent, axis=1, keepdims=True)
    packed = (per * HEAD_DIM, width)
    a_all, (s_fc1_t, s_fc2_t, c_fc1_t) = image_gather(
        probs.astype(BF16).reshape(packed), lines_of, beside_turn
    )
    a_all = a_all.reshape(images, HEAD_DIM, width)

    (glob_out, loc_out, co, ch2, cg, cdu, dc2, cdob, cdo, gram_a, gram_b, cvec2, cbias) = call(
        functools.partial(channel_kernel, globs), chunks, scalars,
        (a_all, cc1, cp, dout, cdg, cvec0, *c_vecs, c_fc1_bias.reshape(1, -1), c_proj, c_fc1,
         c_fc1_t, c_fc2),
        [gram_spec, lines(width), tokens(width, 2), tokens(width), tokens(hidden),
         hold((16, width)), *c_specs, hold((1, hidden)), w_proj, w_fc1, w_fc2, w_fc2],
        [jax.ShapeDtypeStruct(glob_x.shape, BF16), jax.ShapeDtypeStruct(loc_x.shape, BF16),
         b2(), b2(), b2(hidden), b2(hidden), f3(), b2(), b2(),
         half_sums, half_sums, sh(16, width), sh(1, hidden)],
        [glob_spec, loc_spec, tokens(width), tokens(width), tokens(hidden), tokens(hidden),
         lines(width), tokens(width), tokens(width),
         keep(half_sums.shape), keep(half_sums.shape), keep((16, width)), keep((1, hidden))],
        [s_wide, s_tok, s_valid, s_tok, s_tok, s_flat(hidden),
         s_flat(width), s_gram, s_acc, s_bias, s_vec],
        2 * dense, "channel_mid",
    )

    direct = parts == 4 and lines_of == 4 and 4 * width == hidden
    grads = functools.partial(group_grad, place, lanes=width, lines_of=lines_of, parts=parts)

    def scatter(array, axis):
        return lax.psum_scatter(array, axis, scatter_dimension=0, tiled=True)[0]

    def beside_a1(ready):
        pairs = [(after(cdu, ready), ch2)]
        return grads(pairs, ("side",), "one", blocks=(0, 2), name="c_fc1_grads")[0]

    def beside_a2(ready):
        pairs = [(after(dout, ready), cg)]
        return grads(
            pairs, ("rows",), "one", blocks=(1, 2), base=buffer_a1, name="c_fc2_grads"
        )[0]

    dprobs, buffer_a1 = image_sum(gram_a, gram_b, beside_a1 if direct else None)
    dprobs = dprobs.reshape(per, HEAD_DIM, width)
    dscores = probs * (dprobs - jnp.sum(dprobs * probs, axis=1, keepdims=True))
    ds_all, buffer_a = image_gather(
        dscores.astype(BF16).reshape(packed), lines_of, beside_a2 if direct else None
    )
    ds_all = ds_all.reshape(images, HEAD_DIM, width)
    if direct:
        ds_all, buffer_a = together(ds_all, buffer_a)
        piece_a = scatter(buffer_a, "core")

    (cdp, dmid, cvec1) = call(
        functools.partial(channel_back_kernel, globs), chunks, scalars,
        (a_all, ds_all, cp, cdo, dc2, cc1, mid, *c_vecs, c_qkv),
        [gram_spec, gram_spec, tokens(3 * width), tokens(width), lines(width), lines(width),
         lines(width), *c_specs, w_qkv],
        [b2(3 * width), f3(), sh(16, width)],
        [tokens(3 * width), lines(width), keep((16, width))],
        [s_tok, s_valid, s_flat(width), s_acc, s_vec],
        6 * total * width * width, "channel_back",
    )

    kinds_a, kinds_c = ("side", "rows"), ("cols",)
    kinds_s = ("cols", "cols", "side", "rows", "cols", "vec")
    if direct:
        dmid, piece_a = together(dmid, piece_a)
        piece_a = scatter(piece_a, "img")

    (du, dmb, dob, sdc2, sdo, svec2, sbias) = call(
        functools.partial(hidden_back_kernel, globs), chunks, scalars,
        (c2, c3, gp, dmid, *s_vecs, s_proj, s_fc1_t, s_fc2_t),
        [lines(width), lines(width), tokens(hidden), lines(width), *s_specs, w_proj, w_fc2,
         w_fc1],
        [b2(hidden), b2(), b2(), f3(), b2(), sh(16, width), sh(1, hidden)],
        [tokens(hidden), tokens(width), tokens(width), lines(width), tokens(width),
         keep((16, width)), keep((1, hidden))],
        [s_tok, s_valid, s_flat(width), s_acc, s_bias, s_vec],
        2 * total * width * (2 * hidden + width), "hidden_back",
    )
    if direct:
        mine, other = grads(
            [(cdp, ch1), (cdob, co), (du, h2), (dmb, g), (dob, o),
             (cvec2, cvec1, svec2, cbias, sbias)],
            kinds_s, "pair", name="s_fc_grads",
        )
        sdo, mine, other, piece_a = together(sdo, mine, other, piece_a)
        piece_a = scatter(piece_a, "line")
        got = exchange(other, "core")

    dp, svec3 = window_back(probs_s, p, sdo, 0, 2, None)
    if direct:
        dp, got = together(dp, got)
        keep_a, send_a, keep_b, send_b = halved_core(mine, got)
        got_a, got_b = exchange(send_a, "img", 1), exchange(send_b, "img", 2)
        dp = after(dp, keep_a)
    dp, svec3 = window_back(probs_s, p, sdo, 2, chunks - 2, (dp, svec3))
    if direct:
        mine, other = grads([(dp, h1)], kinds_c, "xor", hint=0, name="s_qkv_grads")
        mine, other, got_a, got_b, piece_a = together(mine, other, got_a, got_b, piece_a)
        quarters_a = quarters(piece_a)
        pieces_c = group_sum_core(mine, other, "c")
        keep_a, send_a, keep_b, send_b = halved_first(keep_a, got_a, keep_b, got_b)
        got_a, got_b = exchange(send_a, "img", 2), exchange(send_b, "img", 1)
        held_c = [pieces_c[0]] + [exchange(pieces_c[d], "img", d) for d in range(1, parts)]
        keep_a, got_a, got_b, first_c = together(keep_a, got_a, got_b, pieces_c[0])
        piece_s = halved_second(keep_a, got_a, keep_b, got_b)
        dp, piece_s = together(dp, piece_s)
        piece_s = scatter(piece_s, "line")

    (glob_grad, loc_grad, svec1) = call(
        functools.partial(first_back_kernel, globs), chunks, scalars,
        (glob_x, loc_x, c1, dp, sdc2, *s_vecs, s_qkv, svec3),
        [glob_spec, loc_spec, lines(width), tokens(3 * width), lines(width), *s_specs, w_qkv,
         hold((16, width))],
        [jax.ShapeDtypeStruct(glob_x.shape, F32), jax.ShapeDtypeStruct(loc_x.shape, F32),
         sh(16, width)],
        [glob_spec, loc_spec, keep((16, width))],
        [s_wide, s_tok, s_tok, s_valid, s_flat(width), s_acc, s_vec],
        6 * total * width * width, "first_back",
    )

    share, col = hidden // groups, width // groups
    if direct:
        cut = (lines_of, -1, width)
        svec1, *quarters_a = together(svec1, *quarters_a)
        vectors = [svec1, exchange(svec1, "core")]
        pieces = sum_with_vectors([v.reshape(cut) for v in held_c], vectors, "c_sum_img")
        piece_c = group_sum_line(pieces, "c")
        quarters_s = quarters(after(piece_s, pieces[0]))
        quarters_c = quarters(piece_c)
        small = [(9, 2, col), (2, col)]
        (c_fc1_g, c_fc2_g, c_qkv_g, c_proj_g, s_fc1_g, s_fc2_g, s_proj_g, s_qkv_g,
         s_ker, s_gain, s_shift, s_bias, c_ker, c_gain, c_shift, c_bias) = group_unpack(
            place,
            [(quarters_a, kinds_a), (quarters_s, kinds_s), (quarters_c, kinds_c + ("late",))],
            [(width, share), (col, hidden), (3 * col, width), (col, width), (width, share),
             (col, hidden), (col, width), (3 * col, width)]
            + small + [(8, col), (1, share)] + small + [(9, col), (1, share)],
            "grads_out",
        )
        s_ker, c_ker = s_ker.transpose(1, 0, 2), c_ker.transpose(1, 0, 2)
        s_bias, c_bias = s_bias.reshape(share), c_bias.reshape(share)
    else:

        def reduced(y, x):
            grad = weight_grad(y, x, "weight_grad")
            mine = lax.psum_scatter(grad, GRP, scatter_dimension=0, tiled=True)
            return lax.psum(mine, "img").astype(F32)

        c_fc1_g, c_proj_g, c_fc2_g = reduced(cdu, ch2).T, reduced(cdob, co), reduced(dout, cg)
        c_qkv_g, s_fc1_g, s_fc2_g = reduced(cdp, ch1), reduced(du, h2).T, reduced(dmb, g)
        s_qkv_g, s_proj_g = reduced(dp, h1), reduced(dob, o)
        rows = [all_sum(v) for v in (cvec2, cvec1, svec2, svec1)]
        c2v, c1v, s2v, s1v = [lax.dynamic_slice(v, (0, me * col), (16, col)) for v in rows]
        c_bias, s_bias = [
            lax.dynamic_slice(all_sum(v)[0], (me * share,), (share,)) for v in (cbias, sbias)
        ]

        def small_grads(first, second, attn):
            kernels = jnp.stack([first[0:9], second[0:9]])
            shifts = [first[9], second[9], first[11], second[11], *attn, second[12], second[13]]
            return kernels, jnp.stack([first[10], second[10]]), jnp.stack(shifts)

        c_ker, c_gain, c_shift = small_grads(c1v, c2v, [c1v[12], c1v[13], c1v[14]])
        s_ker, s_gain, s_shift = small_grads(s1v, s2v, [s1v[12], s1v[14]])
    return (
        glob_out, loc_out, glob_grad, loc_grad,
        s_ker, s_gain, s_shift, s_qkv_g.T, s_proj_g.T, s_fc1_g, s_bias, s_fc2_g.T,
        c_ker, c_gain, c_shift, c_qkv_g.T, c_proj_g.T, c_fc1_g, c_bias, c_fc2_g.T,
    )


def solution(mesh):
    whole = jax.sharding.Mesh(
        mesh.devices.reshape(mesh.shape["img"], mesh.shape["grp"] // 2, 2), ("img", *GRP)
    )
    every = ("img", *GRP)
    maps = P(every, None, None, None)
    weight_outs = (
        P(None, None, GRP), P(None, GRP), P(None, GRP), P(None, GRP), P(None, GRP),
        P(None, GRP), P(GRP), P(None, GRP),
    )
    return jax.shard_map(
        shards,
        mesh=whole,
        in_specs=(maps,) * 4 + (P(every, None), P("img"), P("img")) + (P(),) * 16,
        out_specs=(maps,) * 4 + weight_outs * 2,
        check_vma=False,
    )
```
